32 devices in a mesh: groups: 2 (over x), sector: 16 (over z, y, core).
Axes of the slice: x: 2, y: 2, z: 4, core: 2. Of those that a mesh axis runs over, the one named last changes fastest.
Arguments:
- wavefunction: bfloat16 [64, 256, 256], P(('groups', 'sector')), parts along dimension 0, may hold values from -8 to 8
- lower_states: bfloat16 [3, 64, 256, 256], P(None, ('groups', 'sector')), parts along dimension 1, may hold values from -8 to 8
- left_env: bfloat16 [2944, 256, 256], P(('groups', 'sector')), parts along dimension 0, may hold values from -0.375 to 0.375
- right_env: bfloat16 [2944, 256, 256], P(('groups', 'sector')), parts along dimension 0, may hold values from -0.0546875 to 0.0546875
- term_list: int32 [2944, 2], P(('groups', 'sector')), parts along dimension 0, may hold values from 0 to 31, all different within a row
Outputs:
- residual: float32 [64, 256, 256], P(('groups', 'sector')), parts along dimension 0
- ritz_value: float32 [2], P('groups'), parts along dimension 0
The draws below stay inside these ranges and needn't reach their ends.
There are 2 independent parts, one for each index of `groups`. The reference program is written for one: setup_inputs(seed, part) draws one part's arguments, and reference() takes and returns one part's arrays. A program takes and returns all parts, laid end to end along the dimension named above; each array names one. Nothing has to cross between parts.
Inputs may be any that keep to these rules, and one draw needn't show every extreme that they name: Each row of term_list names a source sector and a different destination sector; every sector appears in some row.
All inputs are finite; a program needn't handle non-finite values.
Results may differ from the reference program's by a relative error of at most 0.0015.
The reference program's roundings to bfloat16 on the way count: a program that leaves them out, or rounds other values in their place, can miss the bound.
Values may be sent and summed in bfloat16 or wider, within the bound.
No kernel may reach another device: no remote copies, remote signals or barrier semaphores. Data moves between devices by JAX's collectives and lax.ppermute only.
A program may use at most 192 MiB of HBM per device.

```python
import jax
import jax.numpy as jnp
from jax import lax

B = 256
SEC_DEV = 2
TERM_DEV = 92
LOWER = 3
SECTORS = 32
TERMS = 1472


def shared_states(key):
    return jax.random.normal(key, (LOWER, SECTORS, B, B), jnp.float32)


def draw_lower_states(key, part):
    base = shared_states(key)
    key = jax.random.fold_in(key, 3)
    extra = jax.random.normal(key, base.shape, jnp.float32)
    return jnp.clip(0.9 * base + 0.45 * extra, -8.0, 8.0).astype(jnp.bfloat16)


def draw_wavefunction(key, part):
    base = shared_states(key)
    key = jax.random.fold_in(key, 5)
    noise = jax.random.normal(key, (SECTORS, B, B), jnp.float32)
    return jnp.clip(0.7 * noise + 0.4 * (base[0] + base[1] + base[2]), -8.0, 8.0).astype(jnp.bfloat16)


def block_scale(rng, shape, shards, low, high):
    loudness, own = 1.0, jax.random.fold_in(rng, 6)
    for position, parts in shards:
        draws = jnp.exp(jax.random.uniform(jax.random.fold_in(own, position), (parts,), jnp.float32, low / len(shards), high / len(shards)))
        loudness = loudness * jnp.repeat(draws, shape[position] // parts).reshape([-1 if axis == position else 1 for axis in range(len(shape))])
    return loudness


def distinct(own_key, rows, count, top, lift):
    ranking = jax.random.permutation(jax.random.fold_in(own_key, 1), count)
    favour = ranking
    for power in range(3):
        favour = favour * favour // count
    favour = favour * lift // count
    tickets = jax.random.randint(jax.random.fold_in(own_key, 2), (rows, count), 0, 4096) + favour
    sure = jax.random.permutation(jax.random.fold_in(own_key, 3), rows)[jnp.arange(count) % rows]
    tickets = jnp.where(jnp.arange(rows)[:, None] == sure[None, :], 1 << 14, tickets)
    priority = tickets * count + jnp.arange(count)
    return lax.top_k(priority.astype(jnp.int32), top)[1].astype(jnp.int32)


def centred(own_key, dims, width, limit, split=(), kind=jnp.bfloat16):
    drawn = width * jax.random.normal(own_key, dims, jnp.float32)
    if split:
        drawn = drawn * block_scale(own_key, dims, split, -0.22, 0.18)
    return jnp.clip(drawn, -limit, limit).astype(kind)


def setup_inputs(seed: int = 0, part: int = 0) -> dict:
    seeds = jax.random.split(jax.random.key(seed), 6)
    part_splits = jax.random.split(jax.random.fold_in(seeds[5], part), 6)
    wavefunction = draw_wavefunction(jax.random.fold_in(jax.random.fold_in(seeds[5], part), 71), part)
    lower_states = draw_lower_states(jax.random.fold_in(jax.random.fold_in(seeds[5], part), 71), part)
    left_env = centred(part_splits[2], (TERMS, B, B), B ** -0.5, 0.375, ((0, 16),))
    right_env = centred(part_splits[3], (TERMS, B, B), (B * TERM_DEV // SEC_DEV) ** -0.5, 0.0546875, ((0, 16),))
    term_list = distinct(part_splits[4], TERMS, SECTORS, 2, 512)
    return dict(wavefunction=wavefunction, lower_states=lower_states, left_env=left_env, right_env=right_env, term_list=term_list)


shift_energy = 2.0


def reference(wavefunction, lower_states, left_env, right_env, term_list):
    def add_term(sigma_sum, term_item):
        left_block, right_block, term_pair = term_item
        source = term_pair[0].astype(jnp.int32)
        target = term_pair[1].astype(jnp.int32)
        psi_block = lax.dynamic_index_in_dim(wavefunction, source, 0, keepdims=False)
        half_block = jnp.dot(left_block, psi_block, preferred_element_type=jnp.float32).astype(jnp.bfloat16)
        product = jnp.dot(half_block, right_block, preferred_element_type=jnp.float32)
        current = lax.dynamic_index_in_dim(sigma_sum, target, 0, keepdims=False)
        sigma_sum = lax.dynamic_update_index_in_dim(sigma_sum, current + product, target, 0)
        return sigma_sum, None

    start_sum = jnp.zeros(wavefunction.shape, jnp.float32)
    sigma_sum = lax.scan(add_term, start_sum, (left_env, right_env, term_list))[0]
    psi_full = wavefunction.astype(jnp.float32)
    lower_full = lower_states.astype(jnp.float32)
    correlation = jnp.sum(lower_full * psi_full[None], axis=(1, 2, 3))
    own_norm = jnp.sum(lower_full * lower_full, axis=(1, 2, 3))
    psi_norm = jnp.sum(psi_full * psi_full)
    coeffs = correlation / own_norm
    deflated = sigma_sum + shift_energy * jnp.sum(coeffs[:, None, None, None] * lower_full, axis=0)
    ritz_value = jnp.sum(psi_full * deflated) / psi_norm
    residual = deflated - ritz_value * psi_full
    return residual, ritz_value.reshape(1)
```

```python
import functools

import jax
import jax.numpy as jnp
from jax import lax
from jax.experimental import pallas as pl
from jax.experimental.pallas import tpu as pltpu
from jax.sharding import PartitionSpec as P

shift_energy = 2.0
CORES = 2


def ring_of(mesh):
    chips = mesh.shape["sector"] // CORES
    rows = 2 if mesh.shape["groups"] == 2 else 1
    cols = chips // rows
    order = [z * rows for z in range(cols)]
    for y in range(1, rows):
        order += [z * rows + y for z in reversed(range(cols))]
    return order


def term_kernel(block, sectors, src_ref, dst_ref, left_ref, right_ref, *rest):
    pieces, rest = rest[: -8], rest[-8:]
    psi_hbm = [p for p in pieces]
    mine_ref, other_ref, cross_ref, psi, acc, psi_sem, out_sem, offs = rest
    step = pl.program_id(0)
    last = pl.num_programs(0) - 1

    @pl.when(step == 0)
    def _():
        at = 0
        copies = []
        for n, piece in enumerate(psi_hbm):
            size = piece.shape[0]
            copies.append(pltpu.make_async_copy(piece, psi.at[pl.ds(at, size)], psi_sem.at[n]))
            at += size
        for copy in copies:
            copy.start()
        acc[...] = jnp.zeros_like(acc)
        for copy in copies:
            copy.wait()

    for t in range(block):
        k = step * block + t
        source, target = src_ref[k], dst_ref[k]
        half = jnp.dot(left_ref[t], psi[source], preferred_element_type=jnp.float32).astype(jnp.bfloat16)
        acc[target] += jnp.dot(half, right_ref[t], preferred_element_type=jnp.float32)

    @pl.when(step == last)
    def _():
        half = sectors // 2
        one = pltpu.make_async_copy(acc.at[pl.ds(0, half)], mine_ref, out_sem.at[0])
        two = pltpu.make_async_copy(acc.at[pl.ds(half, half)], other_ref, out_sem.at[1])
        two.start()
        one.start()

        def add(s, total):
            return total + jnp.sum((acc[s] * psi[s].astype(jnp.float32)).reshape(-1, 8, 256), axis=0)

        total = lax.fori_loop(0, sectors, add, jnp.zeros((8, 256), jnp.float32))
        cross_ref[...] = total[:, :128] + total[:, 128:]
        two.wait()
        one.wait()


def all_terms(src, dst, left, right, pieces, sectors):
    terms, side, _ = left.shape
    block = next(b for b in (4, 2, 1) if terms % b == 0)
    half = sectors // 2
    env = pl.BlockSpec((block, side, side), lambda i, *_: (i, 0, 0))
    return pl.pallas_call(
        functools.partial(term_kernel, block, sectors),
        grid_spec=pltpu.PrefetchScalarGridSpec(
            num_scalar_prefetch=2,
            grid=(terms // block,),
            in_specs=[env, env] + [pl.BlockSpec(memory_space=pl.ANY)] * len(pieces),
            out_specs=[
                pl.BlockSpec(memory_space=pl.ANY),
                pl.BlockSpec(memory_space=pl.ANY),
                pl.BlockSpec((8, 128), lambda i, *_: (0, 0)),
            ],
            scratch_shapes=[
                pltpu.VMEM((sectors, side, side), jnp.bfloat16),
                pltpu.VMEM((sectors, side, side), jnp.float32),
                pltpu.SemaphoreType.DMA((len(pieces),)),
                pltpu.SemaphoreType.DMA((2,)),
                pltpu.SMEM((1,), jnp.int32),
            ],
        ),
        out_shape=[
            jax.ShapeDtypeStruct((half, side, side), jnp.float32),
            jax.ShapeDtypeStruct((half, side, side), jnp.float32),
            jax.ShapeDtypeStruct((8, 128), jnp.float32),
        ],
        compiler_params=pltpu.CompilerParams(
            dimension_semantics=("arbitrary",), vmem_limit_bytes=40 * 1024 * 1024
        ),
        cost_estimate=pl.CostEstimate(
            flops=4 * terms * side**3, bytes_accessed=4 * terms * side * side, transcendentals=0
        ),
    )(src, dst, left, right, *pieces)


def make_per_device(mesh):
    devices = mesh.shape["sector"]
    ring = ring_of(mesh)
    chips = len(ring)
    place = [ring.index(c) for c in range(chips)]

    def shift(by):
        return [
            (ring[p] * CORES + c, ring[(p + by) % chips] * CORES + c) for p in range(chips) for c in range(CORES)
        ]

    to_right, to_left = shift(1), shift(-1)
    swap = [(i, i ^ 1) for i in range(devices)]

    def right(x):
        return lax.ppermute(x, "sector", to_right)

    def left(x):
        return lax.ppermute(x, "sector", to_left)

    def across(x):
        return lax.ppermute(x, "sector", swap)

    def everywhere(sums, tops):
        hop = 1
        while hop < devices:
            pairs = [(i, i ^ hop) for i in range(devices)]
            both = lax.ppermute(jnp.concatenate([sums, tops]), "sector", pairs)
            sums, tops = sums + both[: sums.shape[0]], jnp.maximum(tops, both[sums.shape[0] :])
            hop *= 2
        return sums, tops

    def per_device(wavefunction, lower_states, left_env, right_env, term_list):
        per, side, _ = wavefunction.shape
        sectors = per * devices
        part = per // 2
        me = lax.axis_index("sector")
        my_place, my_core = jnp.asarray(place, jnp.int32)[me // CORES], me % CORES

        def slot(sector):
            chip, core, j = sector // (per * CORES), (sector // per) % CORES, sector % per
            rel = (jnp.asarray(place, jnp.int32)[chip] - my_place) % chips
            return jnp.where(core == my_core, 0, chips * per) + rel * per + j

        src, dst = slot(term_list[:, 0]), slot(term_list[:, 1])

        got = {0: [wavefunction]}
        r = l = wavefunction
        for s in range(1, chips // 2):
            r, l = right(r), left(l)
            got[chips - s], got[s] = [r], [l]
        got[chips // 2] = [right(r[:part]), left(l[part:])]
        own = [piece for rel in range(chips) for piece in got[rel]]
        pieces = own + [across(p) for p in own]

        psi_local = wavefunction.astype(jnp.float32)
        lower_local = lower_states.astype(jnp.float32)
        correlation_part = jnp.sum(lower_local * psi_local[None], axis=(1, 2, 3))
        own_part = jnp.sum(lower_local * lower_local, axis=(1, 2, 3))
        norm_part = jnp.sum(psi_local * psi_local)
        tops = jnp.stack([jnp.max(jnp.abs(a)).astype(jnp.float32) for a in (wavefunction, left_env, right_env)])
        sums, tops = everywhere(jnp.concatenate([correlation_part, own_part, norm_part[None]]), tops)
        lower_count = lower_states.shape[0]
        correlation, own_norm, psi_norm = sums[:lower_count], sums[lower_count : 2 * lower_count], sums[-1]
        bound = 1.02 * left_env.shape[0] * devices * side * side * (tops[0] * tops[1] * tops[2])
        power = jnp.clip(15.0 - jnp.ceil(jnp.log2(jnp.maximum(bound, 1e-30))), -60.0, 90.0)
        scale, unscale = jnp.exp2(power), 1.0 / jnp.exp2(power)

        mine, other, cross = all_terms(src, dst, left_env, right_env, pieces, sectors)
        cross_sum, _ = everywhere(jnp.sum(cross)[None], tops[:1])

        got_other = across(other)
        partial = mine + got_other

        def pack(x):
            return (x * scale).astype(jnp.float16)

        def unpack(x):
            return x.astype(jnp.float32) * unscale

        def chunk(rel):
            return partial[rel % chips * per : (rel % chips + 1) * per]

        far = chunk(chips // 2)
        r, l = right(pack(far[:part])), left(pack(far[part:]))
        zero = jnp.zeros((part, side, side), jnp.float32)
        r, l = jnp.concatenate([unpack(r), zero]), jnp.concatenate([zero, unpack(l)])
        for s in range(chips // 2 - 1, 0, -1):
            r, l = unpack(right(pack(chunk(s) + r))), unpack(left(pack(chunk(-s) + l)))
        sigma_local = chunk(0) + r + l

        coeffs = correlation / own_norm
        deflated = sigma_local + shift_energy * jnp.sum(coeffs[:, None, None, None] * lower_local, axis=0)
        ritz_value = (cross_sum[0] + shift_energy * jnp.sum(coeffs * correlation)) / psi_norm
        residual = deflated - ritz_value * psi_local
        return (residual, ritz_value.reshape(1))

    return per_device


def solution(mesh):
    return jax.shard_map(
        make_per_device(mesh),
        mesh=mesh,
        in_specs=(
            P(("groups", "sector"), None, None),
            P(None, ("groups", "sector"), None, None),
            P(("groups", "sector"), None, None),
            P(("groups", "sector"), None, None),
            P(("groups", "sector"), None),
        ),
        out_specs=(P(("groups", "sector"), None, None), P("groups")),
        check_vma=False,
    )
```

```python
import functools

import jax
import jax.numpy as jnp
from jax import lax
from jax.experimental import pallas as pl
from jax.experimental.pallas import tpu as pltpu
from jax.sharding import PartitionSpec as P

shift_energy = 2.0
CORES = 2
BATCH = 8
KEEP = pl.BlockSpec(memory_space=pltpu.VMEM)
SCALAR = pl.BlockSpec(memory_space=pltpu.SMEM)
INHBM = pl.BlockSpec(memory_space=pltpu.HBM)
ANYWHERE = pl.BlockSpec(memory_space=pl.ANY)


def ring_of(mesh):
    chips = mesh.shape["sector"] // CORES
    rows = 2 if mesh.shape["groups"] == 2 else 1
    cols = chips // rows
    order = [z * rows for z in range(cols)]
    for y in range(1, rows):
        order += [z * rows + y for z in reversed(range(cols))]
    return order


def over(x, n):
    return lax.shift_right_logical(x, n.bit_length() - 1) if n & (n - 1) == 0 else lax.div(x, n)


def left_over(x, n):
    return x & (n - 1) if n & (n - 1) == 0 else lax.rem(x, n)


def starts_of(pieces, psi, starts, sems):
    copies = [
        pltpu.make_async_copy(piece, psi.at[pl.ds(start, piece.shape[0])], sems.at[n])
        for n, (piece, start) in enumerate(zip(pieces, starts))
    ]
    for copy in copies:
        copy.start()
    return copies


def top(ref, start, count, m):
    def body(k, m):
        for row in range(0, ref.shape[1], m.shape[0]):
            m = jnp.maximum(m, jnp.abs(ref[start + k, row : row + m.shape[0], :]))
        return m

    return lax.fori_loop(0, count, body, m)


def batch_of_terms(i, plan_ref, left, right, psi, acc, room=()):
    codes = [plan_ref[i * BATCH + u] for u in range(BATCH)]
    ks = [over(c, 65536) for c in codes]
    if room:
        held, sems = room
        copies = [pltpu.make_async_copy(right.at[k], held.at[u], sems.at[u]) for u, k in enumerate(ks)]
        for copy in copies:
            copy.start()
        for copy in copies:
            copy.wait()
        ks, right = list(zip(ks, range(BATCH))), held
    else:
        ks = list(zip(ks, ks))
    halves = [
        jnp.dot(left[k], psi[left_over(over(c, 256), 256)], preferred_element_type=jnp.float32).astype(jnp.bfloat16)
        for (k, _), c in zip(ks, codes)
    ]
    whole = [jnp.dot(h, right[k], preferred_element_type=jnp.float32) for (_, k), h in zip(ks, halves)]
    for c, w in zip(codes, whole):
        acc[left_over(c, 256)] += w


def plan_kernel(
    shape, tl_hbm, me_ref, left_hbm, psi_hbm, lower_hbm,
    left, vec, acc, psi, plan, bounds, tl_ref, psi_ref, lower_ref, codes, kinds, fill, sems, small_sems,
):
    chips, rows_y, per, cap, empty = shape
    terms, side, _ = left.shape
    lower = lower_ref.shape[0]
    reach = chips // 2
    group = terms // sems.shape[0]
    small = [
        pltpu.make_async_copy(a, b, small_sems.at[n])
        for n, (a, b) in enumerate(((tl_hbm, tl_ref), (psi_hbm, psi_ref), (lower_hbm, lower_ref)))
    ]
    copies = [
        pltpu.make_async_copy(left_hbm.at[pl.ds(g * group, group)], left.at[pl.ds(g * group, group)], sems.at[g])
        for g in range(sems.shape[0])
    ]
    for copy in small + copies:
        copy.start()
    small[0].wait()

    def place(chip):
        if rows_y == 1:
            return chip
        z, y = over(chip, rows_y), left_over(chip, rows_y)
        return jnp.where(y == 0, z, chips - 1 - z)

    me = me_ref[0]
    my_place, my_core = place(over(me, CORES)), left_over(me, CORES)

    def slot(sector):
        chip, core, j = over(sector, per * CORES), left_over(over(sector, per), CORES), left_over(sector, per)
        rel = left_over(place(chip) - my_place + chips, chips)
        return rel, jnp.where(core == my_core, 0, chips * per) + rel * per + j

    for stage in range(reach + 1):
        fill[stage] = 0

    def classify(k, carry):
        rel, src = slot(tl_ref[0, k])
        _, dst = slot(tl_ref[1, k])
        stage = jnp.minimum(rel, chips - rel)
        stage = jnp.where(stage == 1, 2, stage)
        codes[k] = k * 65536 + src * 256 + dst
        kinds[k] = stage
        fill[stage] += 1
        return carry

    lax.fori_loop(0, terms, classify, 0, unroll=4)
    at = jnp.int32(0)
    for stage in range(reach + 1):
        bounds[stage] = at
        count = fill[stage]
        fill[stage] = at * BATCH
        at = at + over(count + (BATCH - 1), BATCH)
    bounds[reach + 1] = at

    def put(k, carry):
        stage = kinds[k]
        plan[fill[stage]] = codes[k]
        fill[stage] += 1
        return carry

    lax.fori_loop(0, terms, put, 0, unroll=4)

    for stage in range(reach + 1):

        def pad(i, carry):
            before = plan[i - 1]
            plan[i] = before - left_over(before, 256) + empty
            return carry

        lax.fori_loop(fill[stage], bounds[stage + 1] * BATCH, pad, 0)

    def zero(i, carry):
        acc[i] = jnp.zeros((side, side), jnp.float32)
        return carry

    lax.fori_loop(0, acc.shape[0], zero, 0)

    def fold(x):
        x = jnp.sum(x.reshape(-1, 8, side), axis=0)
        return jnp.sum(x, axis=0, keepdims=True)

    def rows(j):
        psi = psi_ref[j].astype(jnp.float32)
        low = [lower_ref[i, j].astype(jnp.float32) for i in range(lower)]
        return [fold(x * psi) for x in low] + [fold(x * x) for x in low] + [fold(psi * psi)]

    small[1].wait()
    small[2].wait()
    parts = rows(0)
    for j in range(1, psi_ref.shape[0]):
        parts = [a + b for a, b in zip(parts, rows(j))]
    psi[0, 0:16] = jnp.zeros((16, side), psi.dtype)
    vec[...] = jnp.zeros_like(vec)
    for i, x in enumerate(parts):
        vec[pl.ds(i, 1), :] = sum(x[:, c : c + 128] for c in range(0, side, 128))

    for copy in copies:
        copy.wait()


def first_kernel(starts, empty, plan_ref, bounds_ref, left_ref, right_hbm, *rest):
    count = len(starts)
    pieces, rest = rest[:count], rest[count:]
    _, _, acc, psi, right, sems, right_sems = rest

    def brought(i):
        code = plan_ref[i]
        k = over(code, 65536)
        return left_over(code, 256) != empty, pltpu.make_async_copy(right_hbm.at[k], right.at[k], right_sems.at[k])

    def start(i, carry):
        real, copy = brought(i)

        @pl.when(real)
        def _():
            copy.start()

        return carry

    def wait(i, carry):
        real, copy = brought(i)

        @pl.when(real)
        def _():
            copy.wait()

        return carry

    copies = starts_of(pieces, psi, starts, sems)
    end = bounds_ref[bounds_ref.shape[0] - 1]
    lax.fori_loop(0, end * BATCH, start, 0)
    for copy in copies:
        copy.wait()

    def batch(i, carry):
        lax.fori_loop(i * BATCH, (i + 1) * BATCH, wait, 0)
        batch_of_terms(i, plan_ref, left_ref, right, psi, acc)
        return carry

    lax.fori_loop(0, bounds_ref[1], batch, 0)
    lax.fori_loop(bounds_ref[1] * BATCH, end * BATCH, wait, 0)


def stage_kernel(stage, starts, finish, limit, plan_ref, bounds_ref, left_ref, right_ref, *rest):
    count = len(starts)
    pieces, rest = rest[:count], rest[count:]
    if finish:
        vec_ref, _, _, acc, psi = rest[:5]
        outs, rest = rest[5 : 7 + len(finish)], rest[7 + len(finish) :]
        out_sems, rest = rest[0], rest[1:]
    else:
        _, _, acc, psi, *rest = rest
    sems, *room = rest
    copies = starts_of(pieces, psi, starts, sems)
    for copy in copies:
        copy.wait()

    def batch(i, carry):
        batch_of_terms(i, plan_ref, left_ref, right_ref, psi, acc, room)
        return carry

    lax.fori_loop(bounds_ref[stage], bounds_ref[stage + 1], batch, 0)
    if finish:
        outs, vec, scales = outs[:-2], outs[-2], outs[-1]
        moves = []
        for out, chunks in zip(outs, finish):
            put = 0
            for begin, size in chunks:
                place = out.at[pl.ds(put, size)]
                moves.append(pltpu.make_async_copy(acc.at[pl.ds(begin, size)], place, out_sems.at[len(moves)]))
                put += size
        for move in moves:
            move.start()
        side = psi.shape[1]

        def add(s, total):
            for row in range(0, side, 32):
                total += acc[s, row : row + 32, :] * psi[s, row : row + 32, :].astype(jnp.float32)
            return total

        total = lax.fori_loop(0, psi.shape[0], add, jnp.zeros((32, side), jnp.float32))
        total = jnp.sum(total, axis=0, keepdims=True)
        vec[...] = vec_ref[...]
        vec[pl.ds(vec.shape[0] - 1, 1), :] = sum(total[:, c : c + 128] for c in range(0, side, 128))
        largest = jnp.max(top(psi, 0, psi.shape[0], jnp.zeros((16, side), psi.dtype)).astype(jnp.float32))
        bound = jnp.full((1, 128), limit * largest)
        power = jnp.clip(15.0 - jnp.ceil(jnp.log2(jnp.maximum(bound, 1e-30))), -60.0, 90.0)
        scales[...] = jnp.zeros_like(scales)
        scales[0:1, :] = jnp.exp2(power)
        scales[1:2, :] = 1.0 / jnp.exp2(power)
        for move in moves:
            move.wait()


def make_per_device(mesh):
    devices = mesh.shape["sector"]
    ring = ring_of(mesh)
    chips = len(ring)
    reach = chips // 2
    rows_y = 2 if mesh.shape["groups"] == 2 else 1

    def shift(by):
        return [
            (ring[p] * CORES + c, ring[(p + by) % chips] * CORES + c) for p in range(chips) for c in range(CORES)
        ]

    to_right, to_left = shift(1), shift(-1)

    def right(x):
        return lax.ppermute(x, "sector", to_right)

    def left(x):
        return lax.ppermute(x, "sector", to_left)

    def pair(x, hop):
        return lax.ppermute(x, "sector", [(i, i ^ hop) for i in range(devices)])

    def across(x):
        return pair(x, 1)

    bits = [1 << b for b in range(devices.bit_length() - 1)]

    def per_device(wavefunction, lower_states, left_env, right_env, term_list):
        per, side, _ = wavefunction.shape
        terms = left_env.shape[0]
        sectors = per * devices
        part = per // 2
        lower = lower_states.shape[0]
        base = chips * per
        tie = lax.optimization_barrier
        me = lax.axis_index("sector")

        keep = dict(compiler_params=pltpu.CompilerParams(vmem_limit_bytes=8 * 1024 * 1024))
        stages = reach + 1
        cap = (terms + stages * (BATCH - 1) + BATCH - 1) // BATCH * BATCH
        groups = next(g for g in (4, 2, 1) if terms % g == 0)
        vec_rows = -(-(2 * lower + 2) // 8) * 8
        roomy = sectors * side * side * 4 <= 9 << 20
        left_hbm, right_hbm, psi_hbm, lower_hbm, list_hbm = [
            pltpu.with_memory_space_constraint(x, pltpu.HBM)
            for x in (left_env, right_env, wavefunction, lower_states, term_list.T)
        ]
        vec_shape = jax.ShapeDtypeStruct((vec_rows, 128), jnp.float32)
        acc_shape = pltpu.VMEM((sectors + 1, side, side), jnp.float32)
        psi_shape = pltpu.VMEM((sectors, side, side), wavefunction.dtype)

        def make_plan():
            return pl.pallas_call(
                functools.partial(plan_kernel, (chips, rows_y, per, cap, sectors)),
                in_specs=[INHBM, SCALAR, INHBM, INHBM, INHBM],
                out_specs=[KEEP] * 4 + [SCALAR] * 2,
                out_shape=[
                    pltpu.VMEM(left_env.shape, left_env.dtype),
                    vec_shape,
                    acc_shape,
                    psi_shape,
                    jax.ShapeDtypeStruct((cap,), jnp.int32),
                    jax.ShapeDtypeStruct((stages + 1,), jnp.int32),
                ],
                scratch_shapes=[
                    pltpu.SMEM((2, terms), jnp.int32),
                    pltpu.VMEM(wavefunction.shape, wavefunction.dtype),
                    pltpu.VMEM(lower_states.shape, lower_states.dtype),
                    pltpu.SMEM((terms,), jnp.int32),
                    pltpu.SMEM((terms,), jnp.int32),
                    pltpu.SMEM((stages,), jnp.int32),
                    pltpu.SemaphoreType.DMA((groups,)),
                    pltpu.SemaphoreType.DMA((3,)),
                ],
                cost_estimate=pl.CostEstimate(flops=0, bytes_accessed=12 << 20, transcendentals=0),
                **keep,
            )(list_hbm, me.reshape(1).astype(jnp.int32), left_hbm, psi_hbm, lower_hbm)

        def run_first(pieces, starts, acc, psi):
            n = len(pieces)
            return pl.pallas_call(
                functools.partial(first_kernel, starts, sectors),
                in_specs=[SCALAR, SCALAR, KEEP, INHBM] + [ANYWHERE] * n + [KEEP] * 2,
                out_specs=[KEEP] * 3,
                out_shape=[acc_shape, psi_shape, pltpu.VMEM(right_env.shape, right_env.dtype)],
                input_output_aliases={4 + n: 0, 5 + n: 1},
                scratch_shapes=[pltpu.SemaphoreType.DMA((n,)), pltpu.SemaphoreType.DMA((terms,))],
                cost_estimate=pl.CostEstimate(flops=0, bytes_accessed=12 << 20, transcendentals=0),
                **keep,
            )(plan, bounds, left_vmem, right_hbm, *pieces, acc, psi)

        sets = [[reach], [reach - 1, 1 - reach], [x for s in range(reach - 2, 0, -1) for x in (s, -s)] + [0]]

        def run_stage(stage, pieces, starts, acc, psi, vec=None):
            finish, sizes, more, small = [], [], [], []
            if stage == reach:
                finish = [[(base + rel % chips * per, per) for rel in rels] for rels in sets]
                shape_of = pltpu.VMEM if roomy else jax.ShapeDtypeStruct
                sizes = [shape_of((per * len(rels), side, side), jnp.float32) for rels in sets]
                more, small = [vec], [vec_shape, jax.ShapeDtypeStruct((8, 128), jnp.float32)]
            n, m = len(pieces), len(more)
            scratch = [pltpu.SemaphoreType.DMA((n,))]
            if finish:
                scratch = [pltpu.SemaphoreType.DMA((chips,))] + scratch
            if not roomy:
                scratch += [pltpu.VMEM((BATCH, side, side), right_env.dtype), pltpu.SemaphoreType.DMA((BATCH,))]
            limit = 1.02 * terms * devices * side * side * 0.375 * 0.0546875
            return pl.pallas_call(
                functools.partial(stage_kernel, stage, starts, finish, limit),
                in_specs=[SCALAR, SCALAR, KEEP, KEEP if roomy else INHBM] + [ANYWHERE] * n + [KEEP] * (m + 2),
                out_specs=[KEEP] * 2 + [KEEP if roomy else ANYWHERE] * len(sizes) + [KEEP] * len(small),
                out_shape=[acc_shape, psi_shape] + sizes + small,
                input_output_aliases={4 + n + m: 0, 5 + n + m: 1},
                scratch_shapes=scratch,
                cost_estimate=pl.CostEstimate(
                    flops=4 * side**3 * terms // stages, bytes_accessed=1 << 20, transcendentals=0
                ),
                **keep,
            )(plan, bounds, left_vmem, right_vmem, *pieces, *more, acc, psi)

        r, l, sib = right(wavefunction), left(wavefunction), across(wavefunction)
        left_vmem, vec, acc, psi, plan, bounds = make_plan()
        held, at = [], []
        for s in range(1, reach):
            r, l, acc, psi = tie((r, l, acc, psi))
            rel = [(chips - s) * per, s * per]
            held, at = held + [r, l, across(r), across(l)], at + rel + [base + x for x in rel]
            if s < reach - 1:
                r, l = right(r), left(l)
            else:
                r, l = right(r[:part]), left(l[part:])
            if s == 1 and roomy:
                acc, psi, right_vmem = run_first([wavefunction, sib], [0, base], acc, psi)
            elif s == 1:
                right_vmem = right_hbm
                acc, psi = run_stage(0, [wavefunction, sib], [0, base], acc, psi)
            else:
                acc, psi = run_stage(s, held, at, acc, psi)
                held, at = [], []
        r, l, acc, psi = tie((r, l, acc, psi))
        rel = [reach * per, reach * per + part]
        held, at = held + [r, l, across(r), across(l)], at + rel + [base + x for x in rel]
        acc, psi, *others, vec, scales = run_stage(reach, held, at, acc, psi, vec)
        scale, unscale = scales[0, 0], scales[1, 0]

        got = [across(x) for x in others[:-1]]
        *got, late = tie((*got, others[-1]))
        got.append(across(late))

        def pack(x):
            return (x * scale).astype(jnp.float16)

        def unpack(x):
            return x.astype(jnp.float32) * unscale

        halves = (slice(0, part), slice(part, per))

        def own(rel, half):
            part_of, at = next((n, rels.index(rel)) for n, rels in enumerate(sets) if rel in rels)
            begin = rel % chips * per
            return acc[begin : begin + per][halves[half]] + got[part_of][at * per : (at + 1) * per][halves[half]]

        hops, flying = list(bits), None
        route = [(reach, 0)] + [(d, h) for d in range(reach - 1, 0, -1) for h in (1, 0)]
        went, sent = [], []
        for n, (d, h) in enumerate(route):
            to_r, to_l = own(d, h), own(-d if d < reach else reach, 1 - h)
            if n >= 2:
                back, _ = tie((went[n - 2], sent[n - 1]))
                to_r, to_l = to_r + unpack(back[0]), to_l + unpack(back[1])
            sent.append((pack(to_r), pack(to_l)))
            went.append((right(sent[n][0]), left(sent[n][1])))
            if n % 2 == 0 and hops:
                if flying is not None:
                    flying, _ = tie((flying, sent[n]))
                    vec = vec + flying
                flying = pair(vec, hops.pop(0))
        if flying is not None:
            flying, _ = tie((flying, sent[-1]))
            vec = vec + flying
        for hop in hops:
            vec = vec + pair(vec, hop)
        sums = jnp.sum(vec, axis=1)
        correlation, own_norm, psi_norm = sums[:lower], sums[lower : 2 * lower], sums[2 * lower]
        coeffs = correlation / own_norm
        psi_local = wavefunction.astype(jnp.float32)
        lower_local = lower_states.astype(jnp.float32)
        ritz_value = (sums[-1] + shift_energy * jnp.sum(coeffs * correlation)) / psi_norm
        rest = jnp.concatenate([own(0, 0), own(0, 1)])
        rest = rest + shift_energy * jnp.sum(coeffs[:, None, None, None] * lower_local, axis=0)
        (r1, l0), (r0, l1) = went[-2], went[-1]
        arrived = jnp.concatenate([unpack(r0) + unpack(l0), unpack(r1) + unpack(l1)])
        residual = rest + arrived - ritz_value * psi_local
        return (residual, ritz_value.reshape(1))

    return per_device


def solution(mesh):
    return jax.shard_map(
        make_per_device(mesh),
        mesh=mesh,
        in_specs=(
            P(("groups", "sector"), None, None),
            P(None, ("groups", "sector"), None, None),
            P(("groups", "sector"), None, None),
            P(("groups", "sector"), None, None),
            P(("groups", "sector"), None),
        ),
        out_specs=(P(("groups", "sector"), None, None), P("groups")),
        check_vma=False,
    )
```

```python
import functools

import jax
import jax.numpy as jnp
import numpy as np
from jax import lax
from jax.experimental import pallas as pl
from jax.experimental.pallas import tpu as pltpu
from jax.sharding import PartitionSpec as P

shift_energy = 2.0
CORES = 2
BATCH = 8
SLOTS = 4
KEEP = pl.BlockSpec(memory_space=pltpu.VMEM)
SCALAR = pl.BlockSpec(memory_space=pltpu.SMEM)
INHBM = pl.BlockSpec(memory_space=pltpu.HBM)
ANYWHERE = pl.BlockSpec(memory_space=pl.ANY)


def ring_of(mesh):
    chips = mesh.shape["sector"] // CORES
    rows = 2 if mesh.shape["groups"] == 2 else 1
    cols = chips // rows
    order = [z * rows for z in range(cols)]
    for y in range(1, rows):
        order += [z * rows + y for z in reversed(range(cols))]
    return order


def over(x, n):
    return lax.shift_right_logical(x, n.bit_length() - 1) if n & (n - 1) == 0 else lax.div(x, n)


def left_over(x, n):
    return x & (n - 1) if n & (n - 1) == 0 else lax.rem(x, n)


def starts_of(pieces, psi, starts, sems):
    copies = [
        pltpu.make_async_copy(piece, psi.at[pl.ds(start, piece.shape[0])], sems.at[n])
        for n, (piece, start) in enumerate(zip(pieces, starts))
    ]
    for copy in copies:
        copy.start()
    return copies


def terms_of(begin, end, plan_ref, left_hbm, right_hbm, held, sems, ready, psi, acc):
    def bring(i):
        @pl.when(i < end)
        def _():
            at = left_over(i, SLOTS)
            ks = [over(plan_ref[i * BATCH + u], 65536) for u in range(BATCH)]
            for n, env in enumerate((left_hbm, right_hbm)):
                for u, k in enumerate(ks):
                    pltpu.make_async_copy(env.at[k], held.at[at, n, u], sems.at[at, n]).start()

    def batch(i, carry):
        bring(i + SLOTS - 1)
        at = left_over(i, SLOTS)
        for n in range(2):
            pltpu.make_async_copy(held.at[at, n], held.at[at, n], sems.at[at, n]).wait()
        codes = [plan_ref[i * BATCH + u] for u in range(BATCH)]
        halves = [
            jnp.dot(
                held[at, 0, u], psi[left_over(over(c, 256), 256)], preferred_element_type=jnp.float32
            ).astype(jnp.bfloat16)
            for u, c in enumerate(codes)
        ]
        whole = [jnp.dot(h, held[at, 1, u], preferred_element_type=jnp.float32) for u, h in enumerate(halves)]
        for c, w in zip(codes, whole):
            acc[left_over(c, 256)] += w
        return carry

    for ahead in range(SLOTS - 1):
        bring(begin + ahead)
    for copy in ready:
        copy.wait()
    lax.fori_loop(begin, end, batch, 0)


def plan_kernel(
    shape, tl_hbm, me_ref, psi_hbm, lower_hbm,
    vec, acc, psi, plan, bounds, tl_ref, psi_ref, lower_ref, codes, kinds, fill, small_sems,
):
    chips, rows_y, per, cap, empty = shape
    terms = tl_ref.shape[1]
    side = psi.shape[1]
    lower = lower_ref.shape[0]
    reach = chips // 2
    small = [
        pltpu.make_async_copy(a, b, small_sems.at[n])
        for n, (a, b) in enumerate(((tl_hbm, tl_ref), (psi_hbm, psi_ref), (lower_hbm, lower_ref)))
    ]
    for copy in small:
        copy.start()
    small[0].wait()

    def place(chip):
        if rows_y == 1:
            return chip
        z, y = over(chip, rows_y), left_over(chip, rows_y)
        return jnp.where(y == 0, z, chips - 1 - z)

    me = me_ref[0]
    my_place, my_core = place(over(me, CORES)), left_over(me, CORES)

    def slot(sector):
        chip, core, j = over(sector, per * CORES), left_over(over(sector, per), CORES), left_over(sector, per)
        rel = left_over(place(chip) - my_place + chips, chips)
        return rel, jnp.where(core == my_core, 0, chips * per) + rel * per + j

    for stage in range(reach + 1):
        fill[stage] = 0

    def classify(k, carry):
        rel, src = slot(tl_ref[0, k])
        _, dst = slot(tl_ref[1, k])
        stage = jnp.minimum(rel, chips - rel)
        codes[k] = k * 65536 + src * 256 + dst
        kinds[k] = stage
        fill[stage] += 1
        return carry

    lax.fori_loop(0, terms, classify, 0, unroll=4)
    at = jnp.int32(0)
    for stage in range(reach + 1):
        bounds[stage] = at
        count = fill[stage]
        fill[stage] = at * BATCH
        at = at + over(count + (BATCH - 1), BATCH)
    bounds[reach + 1] = at

    def put(k, carry):
        stage = kinds[k]
        plan[fill[stage]] = codes[k]
        fill[stage] += 1
        return carry

    lax.fori_loop(0, terms, put, 0, unroll=4)

    for stage in range(reach + 1):

        def pad(i, carry):
            before = plan[i - 1]
            plan[i] = before - left_over(before, 256) + empty
            return carry

        lax.fori_loop(fill[stage], bounds[stage + 1] * BATCH, pad, 0)

    def zero(i, carry):
        acc[i] = jnp.zeros(acc.shape[1:], jnp.float32)
        return carry

    lax.fori_loop(0, acc.shape[0], zero, 0)

    def fold(x):
        x = jnp.sum(x.reshape(-1, 8, side), axis=0)
        return jnp.sum(x, axis=0, keepdims=True)

    def rows(j):
        psi = psi_ref[j].astype(jnp.float32)
        low = [lower_ref[i, j].astype(jnp.float32) for i in range(lower)]
        return [fold(x * psi) for x in low] + [fold(x * x) for x in low] + [fold(psi * psi)]

    small[1].wait()
    small[2].wait()
    parts = rows(0)
    for j in range(1, psi_ref.shape[0]):
        parts = [a + b for a, b in zip(parts, rows(j))]
    psi[0, 0:16] = jnp.zeros((16, side), psi.dtype)
    vec[...] = jnp.zeros_like(vec)
    for i, x in enumerate(parts):
        vec[pl.ds(i, 1), :] = sum(x[:, c : c + 128] for c in range(0, side, 128))


def stage_kernel(stage, starts, finish, limit, digit, plan_ref, bounds_ref, left_hbm, right_hbm, *rest):
    count = len(starts)
    pieces, rest = rest[:count], rest[count:]
    if finish:
        vec_ref, digit_ref, _, _, acc, psi = rest[:6]
        outs, rest = rest[6 : 6 + len(finish)], rest[6 + len(finish) :]
        scales, digits_ref, vec, out_sems, *rest = rest
    else:
        _, _, acc, psi, *rest = rest
    sems, held, env_sems = rest
    copies = starts_of(pieces, psi, starts, sems)
    begin, end = bounds_ref[stage], bounds_ref[stage + 1]
    terms_of(begin, end, plan_ref, left_hbm, right_hbm, held, env_sems, copies, psi, acc)
    if finish:
        side = psi.shape[1]

        def add(s, carry):
            total, m = carry
            for row in range(0, side, 32):
                piece = psi[s, row : row + 32, :]
                total += acc[s, row : row + 32, :] * piece.astype(jnp.float32)
                m = jnp.maximum(m, jnp.abs(piece))
            return total, m

        moves = []
        for out, chunks in zip(outs, finish):
            put = 0
            for begin, size in chunks:
                place = out.at[pl.ds(put, size), pl.ds(0, side)]
                moves.append(pltpu.make_async_copy(acc.at[pl.ds(begin, size)], place, out_sems.at[len(moves)]))
                put += size
        for move in moves:
            move.start()
        begin = jnp.zeros((32, side), jnp.float32), jnp.zeros((32, side), psi.dtype)
        total, m = lax.fori_loop(0, psi.shape[0], add, begin)
        total = jnp.sum(total, axis=0, keepdims=True)
        vec[...] = vec_ref[...]
        vec[pl.ds(vec.shape[0] - 1, 1), :] = sum(total[:, c : c + 128] for c in range(0, side, 128))
        small = jnp.sum(vec[...], axis=1, keepdims=True)
        digits = jnp.floor(small * digit_ref[0] + 0.5) - digit * jnp.floor(small * digit_ref[1] + 0.5)

        digits_ref[...] = digits
        for out in outs:
            rows = out.shape[1] - side

            def under(i, carry):
                out[i, pl.ds(side, rows), :] = jnp.zeros((rows, side), jnp.float32)
                out[i, pl.ds(side, vec.shape[0]), pl.ds(0, 128)] = digits
                return carry

            lax.fori_loop(0, out.shape[0], under, 0)
        bound = jnp.full((1, 128), limit * jnp.max(m.astype(jnp.float32)))
        power = jnp.clip(15.0 - jnp.ceil(jnp.log2(jnp.maximum(bound, 1e-30))), -60.0, 90.0)
        scales[...] = jnp.zeros_like(scales)
        scales[0:1, :] = jnp.exp2(power)
        scales[1:2, :] = 1.0 / jnp.exp2(power)
        for move in moves:
            move.wait()


def combine_kernel(slots, acc, other, scales, digits, *outs):
    side = acc.shape[2]
    at = 0
    for out in outs:
        for i in range(out.shape[0]):
            out[i, 0:side] = (acc[slots[at]] + other[at, 0:side]) * scales[0:1, 0:1]
            out[i, side:] = other[at, side:]
            out[i, pl.ds(side, digits.shape[0]), pl.ds(0, 128)] += digits[...]
            at += 1


def finish_kernel(lower, digit_ref, scales, home, r0, r1, l0, l1, lower_ref, psi_ref, residual, ritz):
    side = psi_ref.shape[1]
    part = r0.shape[0]
    rows = -(-(2 * lower + 2) // 8) * 8
    place = (0, pl.ds(side, rows), pl.ds(0, 128))
    sums = jnp.sum((home[place] + r0[place] + l0[place]) * digit_ref[2], axis=1, keepdims=True)
    correlation = [sums[j : j + 1] for j in range(lower)]
    coeffs = [correlation[j] / sums[lower + j : lower + j + 1] for j in range(lower)]
    shifted = shift_energy * sum(c * x for c, x in zip(coeffs, correlation))
    value = (sums[rows - 1 : rows] + shifted) / sums[2 * lower : 2 * lower + 1]
    ritz[0] = jnp.sum(value)
    for s in range(psi_ref.shape[0]):
        r, l, at = (r0, l0, s) if s < part else (r1, l1, s - part)
        sigma = (home[s, 0:side] + r[at, 0:side] + l[at, 0:side]) * scales[1:2, 0:1]
        low = sum(c * lower_ref[j, s].astype(jnp.float32) for j, c in enumerate(coeffs))
        residual[s] = sigma + shift_energy * low - value * psi_ref[s].astype(jnp.float32)


def make_per_device(mesh):
    devices = mesh.shape["sector"]
    ring = ring_of(mesh)
    chips = len(ring)
    reach = chips // 2
    rows_y = 2 if mesh.shape["groups"] == 2 else 1

    def shift(by):
        return [
            (ring[p] * CORES + c, ring[(p + by) % chips] * CORES + c) for p in range(chips) for c in range(CORES)
        ]

    to_right, to_left = shift(1), shift(-1)

    def right(x):
        return lax.ppermute(x, "sector", to_right)

    def left(x):
        return lax.ppermute(x, "sector", to_left)

    def pair(x, hop):
        return lax.ppermute(x, "sector", [(i, i ^ hop) for i in range(devices)])

    def across(x):
        return pair(x, 1)

    def per_device(wavefunction, lower_states, left_env, right_env, term_list):
        per, side, _ = wavefunction.shape
        terms = left_env.shape[0]
        sectors = per * devices
        part = per // 2
        lower = lower_states.shape[0]
        base = chips * per
        tie = lax.optimization_barrier
        me = lax.axis_index("sector")

        keep = dict(compiler_params=pltpu.CompilerParams(vmem_limit_bytes=16 * 1024 * 1024))
        stages = reach + 1
        cap = (terms + stages * (BATCH - 1) + BATCH - 1) // BATCH * BATCH
        vec_rows = -(-(2 * lower + 2) // 8) * 8
        left_hbm, right_hbm, psi_hbm, lower_hbm, list_hbm = [
            pltpu.with_memory_space_constraint(x, pltpu.HBM)
            for x in (left_env, right_env, wavefunction, lower_states, term_list.T)
        ]
        vec_shape = jax.ShapeDtypeStruct((vec_rows, 128), jnp.float32)
        row_shape = jax.ShapeDtypeStruct((8, 128), jnp.float32)
        tall = side + -(-vec_rows // 16) * 16
        acc_shape = pltpu.VMEM((sectors + 1, side, side), jnp.float32)
        digit_bits = 12 - (devices.bit_length() - 1)
        weights = np.zeros((3, vec_rows, 128), np.float32)
        for n in range(144 // digit_bits):
            weight = 2.0 ** (digit_bits * n - 72)
            weights[0, :, n], weights[1, :, n], weights[2, :, n] = 1 / weight, 2.0**-digit_bits / weight, weight
        weights = jnp.asarray(weights)
        psi_shape = pltpu.VMEM((sectors, side, side), wavefunction.dtype)

        def make_plan():
            return pl.pallas_call(
                functools.partial(plan_kernel, (chips, rows_y, per, cap, sectors)),
                in_specs=[INHBM, SCALAR, INHBM, INHBM],
                out_specs=[KEEP] * 3 + [SCALAR] * 2,
                out_shape=[
                    vec_shape,
                    acc_shape,
                    psi_shape,
                    jax.ShapeDtypeStruct((cap,), jnp.int32),
                    jax.ShapeDtypeStruct((stages + 1,), jnp.int32),
                ],
                scratch_shapes=[
                    pltpu.SMEM((2, terms), jnp.int32),
                    pltpu.VMEM(wavefunction.shape, wavefunction.dtype),
                    pltpu.VMEM(lower_states.shape, lower_states.dtype),
                    pltpu.SMEM((terms,), jnp.int32),
                    pltpu.SMEM((terms,), jnp.int32),
                    pltpu.SMEM((stages,), jnp.int32),
                    pltpu.SemaphoreType.DMA((3,)),
                ],
                cost_estimate=pl.CostEstimate(flops=0, bytes_accessed=12 << 20, transcendentals=0),
                **keep,
            )(list_hbm, me.reshape(1).astype(jnp.int32), psi_hbm, lower_hbm)

        route = [(reach, 0)] + [(d, h) for d in range(reach - 1, 0, -1) for h in (1, 0)]
        route_left = [(-d if d < reach else reach, 1 - h) for d, h in route]
        need = [x for both in zip(route, route_left) for x in both] + [(0, 0), (0, 1)]
        sets = [need[:4], need[4:]]

        def run_stage(stage, pieces, starts, acc, psi, vec=None):
            finish, sizes, more, small = [], [], [], []
            if stage == reach:
                finish = [[(base + rel % chips * per + h * part, part) for rel, h in parts] for parts in sets]
                sizes = [pltpu.VMEM((part * len(parts), tall, side), jnp.float32) for parts in sets]
                more, small = [vec, weights], [row_shape, vec_shape]
            n, m = len(pieces), len(more)
            scratch = [pltpu.SemaphoreType.DMA((n,))]
            if finish:
                scratch = [pltpu.VMEM((vec_rows, 128), jnp.float32), pltpu.SemaphoreType.DMA((len(need),))] + scratch
            scratch += [
                pltpu.VMEM((SLOTS, 2, BATCH, side, side), left_env.dtype),
                pltpu.SemaphoreType.DMA((SLOTS, 2)),
            ]
            limit = 1.02 * terms * devices * side * side * 0.375 * 0.0546875
            return pl.pallas_call(
                functools.partial(stage_kernel, stage, starts, finish, limit, 2.0**digit_bits),
                in_specs=[SCALAR, SCALAR, INHBM, INHBM] + [INHBM if x is psi_hbm else ANYWHERE for x in pieces]
                + [KEEP] * (m + 2),
                out_specs=[KEEP] * 2 + [KEEP] * len(sizes) + [KEEP] * len(small),
                out_shape=[acc_shape, psi_shape] + sizes + small,
                input_output_aliases={4 + n + m: 0, 5 + n + m: 1},
                scratch_shapes=scratch,
                cost_estimate=pl.CostEstimate(
                    flops=4 * side**3 * terms // stages, bytes_accessed=1 << 20, transcendentals=0
                ),
                **keep,
            )(plan, bounds, left_hbm, right_hbm, *pieces, *more, acc, psi)

        r, l, sib = right(wavefunction), left(wavefunction), across(wavefunction)
        vec, acc, psi, plan, bounds = make_plan()
        acc, psi = run_stage(0, [psi_hbm, sib], [0, base], acc, psi)
        for s in range(1, reach + 1):
            r, l, acc, psi = tie((r, l, acc, psi))
            rel = [(chips - s) * per, s * per] if s < reach else [reach * per, reach * per + part]
            held, at = [r, l, across(r), across(l)], rel + [base + x for x in rel]
            if s < reach - 1:
                r, l = right(r), left(l)
            elif s < reach:
                r, l = right(r[:part]), left(l[part:])
            if s < reach:
                acc, psi = run_stage(s, held, at, acc, psi)
        acc, psi, *others, scales, digits = run_stage(reach, held, at, acc, psi, vec)

        first = across(others[0])
        first, waiting = tie((first, others[1]))
        got = [first, across(waiting)]
        own = {}
        for parts, there in zip(sets, got):
            keys = [key for key in parts if key[0] != 0]
            shapes = [(part, tall, side)] * len(keys)
            if len(keys) < len(parts):
                shapes.append((per, tall, side))
            slots = [rel % chips * per + h * part + i for rel, h in parts for i in range(part)]
            tiles = pl.pallas_call(
                functools.partial(combine_kernel, slots),
                in_specs=[KEEP] * 4,
                out_specs=[KEEP] * len(shapes),
                out_shape=[jax.ShapeDtypeStruct(shape, jnp.float32) for shape in shapes],
                cost_estimate=pl.CostEstimate(flops=0, bytes_accessed=1 << 20, transcendentals=0),
                **keep,
            )(acc, there, scales, digits)
            own.update(zip(keys, tiles))
            home = tiles[-1]

        went, sent = [], []
        for n, (here, there) in enumerate(zip(route, route_left)):
            to_r, to_l = own[here], own[there]
            if n >= 2:
                back, _ = tie((went[n - 2], sent[n - 1]))
                to_r, to_l = to_r + back[0].astype(jnp.float32), to_l + back[1].astype(jnp.float32)
            sent.append((to_r.astype(jnp.float16), to_l.astype(jnp.float16)))
            went.append((right(sent[n][0]), left(sent[n][1])))
        (r1, l0), (r0, l1) = went[-2], went[-1]
        arrived = [x.astype(jnp.float32) for x in (r0, r1, l0, l1)]
        residual, ritz_value = pl.pallas_call(
            functools.partial(finish_kernel, lower),
            in_specs=[KEEP] * 9,
            out_specs=[KEEP, SCALAR],
            out_shape=[
                jax.ShapeDtypeStruct((per, side, side), jnp.float32),
                jax.ShapeDtypeStruct((1,), jnp.float32),
            ],
            cost_estimate=pl.CostEstimate(flops=0, bytes_accessed=2 << 20, transcendentals=0),
            **keep,
        )(weights, scales, home, *arrived, lower_states, wavefunction)
        return (residual, ritz_value)

    return per_device


def solution(mesh):
    return jax.shard_map(
        make_per_device(mesh),
        mesh=mesh,
        in_specs=(
            P(("groups", "sector"), None, None),
            P(None, ("groups", "sector"), None, None),
            P(("groups", "sector"), None, None),
            P(("groups", "sector"), None, None),
            P(("groups", "sector"), None),
        ),
        out_specs=(P(("groups", "sector"), None, None), P("groups")),
        check_vma=False,
    )
```

```python
import functools

import jax
import jax.numpy as jnp
import numpy as np
from jax import lax
from jax.experimental import pallas as pl
from jax.experimental.pallas import tpu as pltpu
from jax.sharding import PartitionSpec as P

shift_energy = 2.0
CORES = 2
BATCH = 8
SLOTS = 3
KEEP = pl.BlockSpec(memory_space=pltpu.VMEM)
SCALAR = pl.BlockSpec(memory_space=pltpu.SMEM)
INHBM = pl.BlockSpec(memory_space=pltpu.HBM)
ANYWHERE = pl.BlockSpec(memory_space=pl.ANY)


def ring_of(mesh):
    chips = mesh.shape["sector"] // CORES
    rows = 2 if mesh.shape["groups"] == 2 else 1
    cols = chips // rows
    order = [z * rows for z in range(cols)]
    for y in range(1, rows):
        order += [z * rows + y for z in reversed(range(cols))]
    return order


def over(x, n):
    return lax.shift_right_logical(x, n.bit_length() - 1) if n & (n - 1) == 0 else lax.div(x, n)


def left_over(x, n):
    return x & (n - 1) if n & (n - 1) == 0 else lax.rem(x, n)


def starts_of(pieces, psi, starts, sems):
    copies = [
        pltpu.make_async_copy(piece, psi.at[pl.ds(start, piece.shape[0])], sems.at[n])
        for n, (piece, start) in enumerate(zip(pieces, starts))
    ]
    for copy in copies:
        copy.start()
    return copies


def terms_of(begin, end, plan_ref, left, right_hbm, held, sems, ready, psi, acc):
    def bring(i):
        @pl.when(i < end)
        def _():
            at = left_over(i, SLOTS)
            ks = [over(plan_ref[i * BATCH + u], 65536) for u in range(BATCH)]
            for u, k in enumerate(ks):
                pltpu.make_async_copy(right_hbm.at[k], held.at[at, u], sems.at[at]).start()

    def batch(i, carry):
        bring(i + SLOTS - 1)
        at = left_over(i, SLOTS)
        pltpu.make_async_copy(held.at[at], held.at[at], sems.at[at]).wait()
        codes = [plan_ref[i * BATCH + u] for u in range(BATCH)]
        halves = [
            jnp.dot(
                left[over(c, 65536)], psi[left_over(over(c, 256), 256)], preferred_element_type=jnp.float32
            ).astype(jnp.bfloat16)
            for c in codes
        ]
        whole = [jnp.dot(h, held[at, u], preferred_element_type=jnp.float32) for u, h in enumerate(halves)]
        for c, w in zip(codes, whole):
            acc[left_over(c, 256)] += w
        return carry

    for ahead in range(SLOTS - 1):
        bring(begin + ahead)
    for copy in ready:
        copy.wait()
    lax.fori_loop(begin, end, batch, 0)


def plan_kernel(
    shape, tl_hbm, me_ref, psi_hbm, lower_hbm, left_hbm,
    left, vec, acc, psi, plan, bounds, tl_ref, psi_ref, lower_ref, codes, kinds, fill, small_sems, sems,
):
    chips, rows_y, per, cap, empty = shape
    terms = tl_ref.shape[1]
    side = psi.shape[1]
    lower = lower_ref.shape[0]
    reach = chips // 2
    small = [
        pltpu.make_async_copy(a, b, small_sems.at[n])
        for n, (a, b) in enumerate(((tl_hbm, tl_ref), (psi_hbm, psi_ref), (lower_hbm, lower_ref)))
    ]
    group = terms // sems.shape[0]
    copies = [
        pltpu.make_async_copy(left_hbm.at[pl.ds(g * group, group)], left.at[pl.ds(g * group, group)], sems.at[g])
        for g in range(sems.shape[0])
    ]
    for copy in small + copies:
        copy.start()
    small[0].wait()

    def place(chip):
        if rows_y == 1:
            return chip
        z, y = over(chip, rows_y), left_over(chip, rows_y)
        return jnp.where(y == 0, z, chips - 1 - z)

    me = me_ref[0]
    my_place, my_core = place(over(me, CORES)), left_over(me, CORES)

    def slot(sector):
        chip, core, j = over(sector, per * CORES), left_over(over(sector, per), CORES), left_over(sector, per)
        rel = left_over(place(chip) - my_place + chips, chips)
        return rel, jnp.where(core == my_core, 0, chips * per) + rel * per + j

    for stage in range(reach + 1):
        fill[stage] = 0

    def classify(k, carry):
        rel, src = slot(tl_ref[0, k])
        _, dst = slot(tl_ref[1, k])
        stage = jnp.maximum(jnp.minimum(rel, chips - rel), 1)
        codes[k] = k * 65536 + src * 256 + dst
        kinds[k] = stage
        fill[stage] += 1
        return carry

    lax.fori_loop(0, terms, classify, 0, unroll=4)
    at = jnp.int32(0)
    for stage in range(reach + 1):
        bounds[stage] = at
        count = fill[stage]
        fill[stage] = at * BATCH
        at = at + over(count + (BATCH - 1), BATCH)
    bounds[reach + 1] = at

    def put(k, carry):
        stage = kinds[k]
        plan[fill[stage]] = codes[k]
        fill[stage] += 1
        return carry

    lax.fori_loop(0, terms, put, 0, unroll=4)

    for stage in range(reach + 1):

        def pad(i, carry):
            before = plan[i - 1]
            plan[i] = before - left_over(before, 256) + empty
            return carry

        lax.fori_loop(fill[stage], bounds[stage + 1] * BATCH, pad, 0)

    def zero(i, carry):
        acc[i] = jnp.zeros(acc.shape[1:], jnp.float32)
        return carry

    lax.fori_loop(0, acc.shape[0], zero, 0)

    def fold(x):
        x = jnp.sum(x.reshape(-1, 8, side), axis=0)
        return jnp.sum(x, axis=0, keepdims=True)

    def rows(j):
        psi = psi_ref[j].astype(jnp.float32)
        low = [lower_ref[i, j].astype(jnp.float32) for i in range(lower)]
        return [fold(x * psi) for x in low] + [fold(x * x) for x in low] + [fold(psi * psi)]

    small[1].wait()
    small[2].wait()
    parts = rows(0)
    for j in range(1, psi_ref.shape[0]):
        parts = [a + b for a, b in zip(parts, rows(j))]
    psi[0, 0:16] = jnp.zeros((16, side), psi.dtype)
    vec[...] = jnp.zeros_like(vec)
    for i, x in enumerate(parts):
        vec[pl.ds(i, 1), :] = sum(x[:, c : c + 128] for c in range(0, side, 128))
    for copy in copies:
        copy.wait()


def stage_kernel(stage, starts, finish, limit, digit, plan_ref, bounds_ref, left, right_hbm, *rest):
    count = len(starts)
    pieces, rest = rest[:count], rest[count:]
    if finish:
        vec_ref, digit_ref, _, _, acc, psi = rest[:6]
        outs, rest = rest[6 : 6 + len(finish)], rest[6 + len(finish) :]
        scales, digits_ref, vec, out_sems, *rest = rest
    else:
        _, _, acc, psi, *rest = rest
    sems, held, env_sems = rest
    copies = starts_of(pieces, psi, starts, sems)
    begin, end = bounds_ref[stage], bounds_ref[stage + 1]
    terms_of(begin, end, plan_ref, left, right_hbm, held, env_sems, copies, psi, acc)
    if finish:
        side = psi.shape[1]

        def add(s, carry):
            total, m = carry
            for row in range(0, side, 32):
                piece = psi[s, row : row + 32, :]
                total += acc[s, row : row + 32, :] * piece.astype(jnp.float32)
                m = jnp.maximum(m, jnp.abs(piece))
            return total, m

        moves = []
        for out, chunks in zip(outs, finish):
            put = 0
            for begin, size in chunks:
                place = out.at[pl.ds(put, size), pl.ds(0, side)]
                moves.append(pltpu.make_async_copy(acc.at[pl.ds(begin, size)], place, out_sems.at[len(moves)]))
                put += size
        for move in moves:
            move.start()
        begin = jnp.zeros((32, side), jnp.float32), jnp.zeros((32, side), psi.dtype)
        total, m = lax.fori_loop(0, psi.shape[0], add, begin)
        total = jnp.sum(total, axis=0, keepdims=True)
        vec[...] = vec_ref[...]
        vec[pl.ds(vec.shape[0] - 1, 1), :] = sum(total[:, c : c + 128] for c in range(0, side, 128))
        small = jnp.sum(vec[...], axis=1, keepdims=True)
        digits = jnp.floor(small * digit_ref[0] + 0.5) - digit * jnp.floor(small * digit_ref[1] + 0.5)

        digits_ref[...] = digits
        for out in outs:
            rows = out.shape[1] - side

            def under(i, carry):
                out[i, pl.ds(side, rows), :] = jnp.zeros((rows, side), jnp.float32)
                out[i, pl.ds(side, vec.shape[0]), pl.ds(0, 128)] = digits
                return carry

            lax.fori_loop(0, out.shape[0], under, 0)
        bound = jnp.full((1, 128), limit * jnp.max(m.astype(jnp.float32)))
        power = jnp.clip(15.0 - jnp.ceil(jnp.log2(jnp.maximum(bound, 1e-30))), -60.0, 90.0)
        scales[...] = jnp.zeros_like(scales)
        scales[0:1, :] = jnp.exp2(power)
        scales[1:2, :] = 1.0 / jnp.exp2(power)
        for move in moves:
            move.wait()


def combine_kernel(slots, acc, other, scales, digits, *outs):
    side = acc.shape[2]
    at = 0
    for out in outs:
        for i in range(out.shape[0]):
            out[i, 0:side] = (acc[slots[at]] + other[at, 0:side]) * scales[0:1, 0:1]
            out[i, side:] = other[at, side:]
            out[i, pl.ds(side, digits.shape[0]), pl.ds(0, 128)] += digits[...]
            at += 1


def finish_kernel(lower, digit_ref, scales, home, r0, r1, l0, l1, lower_ref, psi_ref, residual, ritz):
    side = psi_ref.shape[1]
    part = r0.shape[0]
    rows = -(-(2 * lower + 2) // 8) * 8
    place = (0, pl.ds(side, rows), pl.ds(0, 128))
    sums = jnp.sum((home[place] + r0[place] + l0[place]) * digit_ref[2], axis=1, keepdims=True)
    correlation = [sums[j : j + 1] for j in range(lower)]
    coeffs = [correlation[j] / sums[lower + j : lower + j + 1] for j in range(lower)]
    shifted = shift_energy * sum(c * x for c, x in zip(coeffs, correlation))
    value = (sums[rows - 1 : rows] + shifted) / sums[2 * lower : 2 * lower + 1]
    ritz[0] = jnp.sum(value)
    for s in range(psi_ref.shape[0]):
        r, l, at = (r0, l0, s) if s < part else (r1, l1, s - part)
        sigma = (home[s, 0:side] + r[at, 0:side] + l[at, 0:side]) * scales[1:2, 0:1]
        low = sum(c * lower_ref[j, s].astype(jnp.float32) for j, c in enumerate(coeffs))
        residual[s] = sigma + shift_energy * low - value * psi_ref[s].astype(jnp.float32)


def make_per_device(mesh):
    devices = mesh.shape["sector"]
    ring = ring_of(mesh)
    chips = len(ring)
    reach = chips // 2
    rows_y = 2 if mesh.shape["groups"] == 2 else 1

    def shift(by):
        return [
            (ring[p] * CORES + c, ring[(p + by) % chips] * CORES + c) for p in range(chips) for c in range(CORES)
        ]

    to_right, to_left = shift(1), shift(-1)

    def right(x):
        return lax.ppermute(x, "sector", to_right)

    def left(x):
        return lax.ppermute(x, "sector", to_left)

    def pair(x, hop):
        return lax.ppermute(x, "sector", [(i, i ^ hop) for i in range(devices)])

    def across(x):
        return pair(x, 1)

    def per_device(wavefunction, lower_states, left_env, right_env, term_list):
        per, side, _ = wavefunction.shape
        terms = left_env.shape[0]
        sectors = per * devices
        part = per // 2
        lower = lower_states.shape[0]
        base = chips * per
        tie = lax.optimization_barrier
        me = lax.axis_index("sector")

        keep = dict(compiler_params=pltpu.CompilerParams(vmem_limit_bytes=9 * 1024 * 1024))
        stages = reach + 1
        cap = (terms + stages * (BATCH - 1) + BATCH - 1) // BATCH * BATCH
        groups = next(g for g in (4, 2, 1) if terms % g == 0)
        vec_rows = -(-(2 * lower + 2) // 8) * 8
        left_hbm, right_hbm, psi_hbm, lower_hbm, list_hbm = [
            pltpu.with_memory_space_constraint(x, pltpu.HBM)
            for x in (left_env, right_env, wavefunction, lower_states, term_list.T)
        ]
        vec_shape = jax.ShapeDtypeStruct((vec_rows, 128), jnp.float32)
        row_shape = jax.ShapeDtypeStruct((8, 128), jnp.float32)
        tall = side + -(-vec_rows // 16) * 16
        acc_shape = pltpu.VMEM((sectors + 1, side, side), jnp.float32)
        digit_bits = 12 - (devices.bit_length() - 1)
        weights = np.zeros((3, vec_rows, 128), np.float32)
        for n in range(144 // digit_bits):
            weight = 2.0 ** (digit_bits * n - 72)
            weights[0, :, n], weights[1, :, n], weights[2, :, n] = 1 / weight, 2.0**-digit_bits / weight, weight
        weights = jnp.asarray(weights)
        psi_shape = pltpu.VMEM((sectors, side, side), wavefunction.dtype)

        def make_plan():
            return pl.pallas_call(
                functools.partial(plan_kernel, (chips, rows_y, per, cap, sectors)),
                in_specs=[INHBM, SCALAR, INHBM, INHBM, INHBM],
                out_specs=[KEEP] * 4 + [SCALAR] * 2,
                out_shape=[
                    pltpu.VMEM(left_env.shape, left_env.dtype),
                    vec_shape,
                    acc_shape,
                    psi_shape,
                    jax.ShapeDtypeStruct((cap,), jnp.int32),
                    jax.ShapeDtypeStruct((stages + 1,), jnp.int32),
                ],
                scratch_shapes=[
                    pltpu.SMEM((2, terms), jnp.int32),
                    pltpu.VMEM(wavefunction.shape, wavefunction.dtype),
                    pltpu.VMEM(lower_states.shape, lower_states.dtype),
                    pltpu.SMEM((terms,), jnp.int32),
                    pltpu.SMEM((terms,), jnp.int32),
                    pltpu.SMEM((stages,), jnp.int32),
                    pltpu.SemaphoreType.DMA((3,)),
                    pltpu.SemaphoreType.DMA((groups,)),
                ],
                cost_estimate=pl.CostEstimate(flops=0, bytes_accessed=12 << 20, transcendentals=0),
                **keep,
            )(list_hbm, me.reshape(1).astype(jnp.int32), psi_hbm, lower_hbm, left_hbm)

        route = [(reach, 0)] + [(d, h) for d in range(reach - 1, 0, -1) for h in (1, 0)]
        route_left = [(-d if d < reach else reach, 1 - h) for d, h in route]
        need = [x for both in zip(route, route_left) for x in both] + [(0, 0), (0, 1)]
        sets = [need[:4], need[4:]]

        def run_stage(stage, pieces, starts, acc, psi, vec=None):
            finish, sizes, more, small = [], [], [], []
            if stage == reach:
                finish = [[(base + rel % chips * per + h * part, part) for rel, h in parts] for parts in sets]
                sizes = [pltpu.VMEM((part * len(parts), tall, side), jnp.float32) for parts in sets]
                more, small = [vec, weights], [row_shape, vec_shape]
            n, m = len(pieces), len(more)
            scratch = [pltpu.SemaphoreType.DMA((n,))]
            if finish:
                scratch = [pltpu.VMEM((vec_rows, 128), jnp.float32), pltpu.SemaphoreType.DMA((len(need),))] + scratch
            scratch += [
                pltpu.VMEM((SLOTS, BATCH, side, side), right_env.dtype),
                pltpu.SemaphoreType.DMA((SLOTS,)),
            ]
            limit = 1.02 * terms * devices * side * side * 0.375 * 0.0546875
            return pl.pallas_call(
                functools.partial(stage_kernel, stage, starts, finish, limit, 2.0**digit_bits),
                in_specs=[SCALAR, SCALAR, KEEP, INHBM] + [INHBM if x is psi_hbm else ANYWHERE for x in pieces]
                + [KEEP] * (m + 2),
                out_specs=[KEEP] * 2 + [KEEP] * len(sizes) + [KEEP] * len(small),
                out_shape=[acc_shape, psi_shape] + sizes + small,
                input_output_aliases={4 + n + m: 0, 5 + n + m: 1},
                scratch_shapes=scratch,
                cost_estimate=pl.CostEstimate(
                    flops=4 * side**3 * terms // stages, bytes_accessed=1 << 20, transcendentals=0
                ),
                **keep,
            )(plan, bounds, left_vmem, right_hbm, *pieces, *more, acc, psi)

        r, l, sib = right(wavefunction), left(wavefunction), across(wavefunction)
        left_vmem, vec, acc, psi, plan, bounds = make_plan()
        late, late_at = [psi_hbm, sib], [0, base]
        for s in range(1, reach + 1):
            r, l, acc, psi = tie((r, l, acc, psi))
            rel = [(chips - s) * per, s * per] if s < reach else [reach * per, reach * per + part]
            held, at = late + [r, l, across(r), across(l)], late_at + rel + [base + x for x in rel]
            late, late_at = [], []
            if s < reach - 1:
                r, l = right(r), left(l)
            elif s < reach:
                r, l = right(r[:part]), left(l[part:])
            if s < reach:
                acc, psi = run_stage(s, held, at, acc, psi)
        acc, psi, *others, scales, digits = run_stage(reach, held, at, acc, psi, vec)

        first = across(others[0])
        first, waiting = tie((first, others[1]))
        got = [first, across(waiting)]
        own = {}
        for parts, there in zip(sets, got):
            keys = [key for key in parts if key[0] != 0]
            shapes = [(part, tall, side)] * len(keys)
            if len(keys) < len(parts):
                shapes.append((per, tall, side))
            slots = [rel % chips * per + h * part + i for rel, h in parts for i in range(part)]
            tiles = pl.pallas_call(
                functools.partial(combine_kernel, slots),
                in_specs=[KEEP] * 4,
                out_specs=[KEEP] * len(shapes),
                out_shape=[jax.ShapeDtypeStruct(shape, jnp.float32) for shape in shapes],
                cost_estimate=pl.CostEstimate(flops=0, bytes_accessed=1 << 20, transcendentals=0),
                **keep,
            )(acc, there, scales, digits)
            own.update(zip(keys, tiles))
            home = tiles[-1]

        went, sent = [], []
        for n, (here, there) in enumerate(zip(route, route_left)):
            to_r, to_l = own[here], own[there]
            if n >= 2:
                back, _ = tie((went[n - 2], sent[n - 1]))
                to_r, to_l = to_r + back[0].astype(jnp.float32), to_l + back[1].astype(jnp.float32)
            sent.append((to_r.astype(jnp.float16), to_l.astype(jnp.float16)))
            went.append((right(sent[n][0]), left(sent[n][1])))
        (r1, l0), (r0, l1) = went[-2], went[-1]
        arrived = [x.astype(jnp.float32) for x in (r0, r1, l0, l1)]
        residual, ritz_value = pl.pallas_call(
            functools.partial(finish_kernel, lower),
            in_specs=[KEEP] * 9,
            out_specs=[KEEP, SCALAR],
            out_shape=[
                jax.ShapeDtypeStruct((per, side, side), jnp.float32),
                jax.ShapeDtypeStruct((1,), jnp.float32),
            ],
            cost_estimate=pl.CostEstimate(flops=0, bytes_accessed=2 << 20, transcendentals=0),
            **keep,
        )(weights, scales, home, *arrived, lower_states, wavefunction)
        return (residual, ritz_value)

    return per_device


def solution(mesh):
    return jax.shard_map(
        make_per_device(mesh),
        mesh=mesh,
        in_specs=(
            P(("groups", "sector"), None, None),
            P(None, ("groups", "sector"), None, None),
            P(("groups", "sector"), None, None),
            P(("groups", "sector"), None, None),
            P(("groups", "sector"), None),
        ),
        out_specs=(P(("groups", "sector"), None, None), P("groups")),
        check_vma=False,
    )
```

```python
import functools

import jax
import jax.numpy as jnp
import numpy as np
from jax import lax
from jax.experimental import pallas as pl
from jax.experimental.pallas import tpu as pltpu
from jax.sharding import PartitionSpec as P

shift_energy = 2.0
CORES = 2
BATCH = 8
SLOTS = 3
KEEP = pl.BlockSpec(memory_space=pltpu.VMEM)
SCALAR = pl.BlockSpec(memory_space=pltpu.SMEM)
INHBM = pl.BlockSpec(memory_space=pltpu.HBM)
ANYWHERE = pl.BlockSpec(memory_space=pl.ANY)


def ring_of(mesh):
    chips = mesh.shape["sector"] // CORES
    rows = 2 if mesh.shape["groups"] == 2 else 1
    cols = chips // rows
    order = [z * rows for z in range(cols)]
    for y in range(1, rows):
        order += [z * rows + y for z in reversed(range(cols))]
    return order


def over(x, n):
    return lax.shift_right_logical(x, n.bit_length() - 1) if n & (n - 1) == 0 else lax.div(x, n)


def left_over(x, n):
    return x & (n - 1) if n & (n - 1) == 0 else lax.rem(x, n)


def starts_of(pieces, psi, starts, sems):
    copies = [
        pltpu.make_async_copy(piece, psi.at[pl.ds(start, piece.shape[0])], sems.at[n])
        for n, (piece, start) in enumerate(zip(pieces, starts))
    ]
    for copy in copies:
        copy.start()
    return copies


def terms_of(begin, end, plan_ref, left, right_hbm, held, sems, ready, psi, acc):
    def bring(i):
        @pl.when(i < end)
        def _():
            at = left_over(i, SLOTS)
            ks = [over(plan_ref[i * BATCH + u], 65536) for u in range(BATCH)]
            for u, k in enumerate(ks):
                pltpu.make_async_copy(right_hbm.at[k], held.at[at, u], sems.at[at]).start()

    def batch(i, carry):
        bring(i + SLOTS - 1)
        at = left_over(i, SLOTS)
        pltpu.make_async_copy(held.at[at], held.at[at], sems.at[at]).wait()
        codes = [plan_ref[i * BATCH + u] for u in range(BATCH)]
        halves = [
            jnp.dot(
                left[over(c, 65536)], psi[left_over(over(c, 256), 256)], preferred_element_type=jnp.float32
            ).astype(jnp.bfloat16)
            for c in codes
        ]
        whole = [jnp.dot(h, held[at, u], preferred_element_type=jnp.float32) for u, h in enumerate(halves)]
        for c, w in zip(codes, whole):
            acc[left_over(c, 256)] += w
        return carry

    for ahead in range(SLOTS - 1):
        bring(begin + ahead)
    for copy in ready:
        copy.wait()
    lax.fori_loop(begin, end, batch, 0)


def plan_kernel(
    shape, tl_hbm, me_ref, psi_hbm, lower_hbm, left_hbm,
    left, vec, acc, psi, plan, bounds, tl_ref, psi_ref, lower_ref, codes, kinds, fill, small_sems, sems,
):
    chips, rows_y, per, cap, empty = shape
    terms = tl_ref.shape[1]
    side = psi.shape[1]
    lower = lower_ref.shape[0]
    reach = chips // 2
    small = [
        pltpu.make_async_copy(a, b, small_sems.at[n])
        for n, (a, b) in enumerate(((tl_hbm, tl_ref), (psi_hbm, psi_ref), (lower_hbm, lower_ref)))
    ]
    group = terms // sems.shape[0]
    copies = [
        pltpu.make_async_copy(left_hbm.at[pl.ds(g * group, group)], left.at[pl.ds(g * group, group)], sems.at[g])
        for g in range(sems.shape[0])
    ]
    for copy in small + copies:
        copy.start()
    small[0].wait()

    def place(chip):
        if rows_y == 1:
            return chip
        z, y = over(chip, rows_y), left_over(chip, rows_y)
        return jnp.where(y == 0, z, chips - 1 - z)

    me = me_ref[0]
    my_place, my_core = place(over(me, CORES)), left_over(me, CORES)

    def slot(sector):
        chip, core, j = over(sector, per * CORES), left_over(over(sector, per), CORES), left_over(sector, per)
        rel = left_over(place(chip) - my_place + chips, chips)
        return rel, jnp.where(core == my_core, 0, chips * per) + rel * per + j

    for stage in range(reach + 1):
        fill[stage] = 0

    def classify(k, carry):
        rel, src = slot(tl_ref[0, k])
        _, dst = slot(tl_ref[1, k])
        stage = jnp.maximum(jnp.minimum(rel, chips - rel), 1)
        codes[k] = k * 65536 + src * 256 + dst
        kinds[k] = stage
        fill[stage] += 1
        return carry

    lax.fori_loop(0, terms, classify, 0, unroll=4)
    at = jnp.int32(0)
    for stage in range(reach + 1):
        bounds[stage] = at
        count = fill[stage]
        fill[stage] = at * BATCH
        at = at + over(count + (BATCH - 1), BATCH)
    bounds[reach + 1] = at

    def put(k, carry):
        stage = kinds[k]
        plan[fill[stage]] = codes[k]
        fill[stage] += 1
        return carry

    lax.fori_loop(0, terms, put, 0, unroll=4)

    for stage in range(reach + 1):

        def pad(i, carry):
            before = plan[i - 1]
            plan[i] = before - left_over(before, 256) + empty
            return carry

        lax.fori_loop(fill[stage], bounds[stage + 1] * BATCH, pad, 0)

    def zero(i, carry):
        acc[i] = jnp.zeros(acc.shape[1:], jnp.float32)
        return carry

    lax.fori_loop(0, acc.shape[0], zero, 0)

    def fold(x):
        x = jnp.sum(x.reshape(-1, 8, side), axis=0)
        return jnp.sum(x, axis=0, keepdims=True)

    def rows(j):
        psi = psi_ref[j].astype(jnp.float32)
        low = [lower_ref[i, j].astype(jnp.float32) for i in range(lower)]
        return [fold(x * psi) for x in low] + [fold(x * x) for x in low] + [fold(psi * psi)]

    small[1].wait()
    small[2].wait()
    parts = rows(0)
    for j in range(1, psi_ref.shape[0]):
        parts = [a + b for a, b in zip(parts, rows(j))]
    psi[0, 0:16] = jnp.zeros((16, side), psi.dtype)
    vec[...] = jnp.zeros_like(vec)
    for i, x in enumerate(parts):
        vec[pl.ds(i, 1), :] = sum(x[:, c : c + 128] for c in range(0, side, 128))
    for copy in copies:
        copy.wait()


def stage_kernel(stage, starts, finish, limit, digit, plan_ref, bounds_ref, left, right_hbm, *rest):
    count = len(starts)
    pieces, rest = rest[:count], rest[count:]
    if finish:
        vec_ref, digit_ref, _, _, acc, psi = rest[:6]
        outs, rest = rest[6 : 6 + len(finish)], rest[6 + len(finish) :]
        scales, digits_ref, vec, out_sems, *rest = rest
    else:
        _, _, acc, psi, *rest = rest
    sems, held, env_sems = rest
    copies = starts_of(pieces, psi, starts, sems)
    begin, end = bounds_ref[stage], bounds_ref[stage + 1]
    terms_of(begin, end, plan_ref, left, right_hbm, held, env_sems, copies, psi, acc)
    if finish:
        side = psi.shape[1]

        def add(s, carry):
            total, m = carry
            for row in range(0, side, 32):
                piece = psi[s, row : row + 32, :]
                total += acc[s, row : row + 32, :] * piece.astype(jnp.float32)
                m = jnp.maximum(m, jnp.abs(piece))
            return total, m

        moves = []
        for out, chunks in zip(outs, finish):
            put = 0
            for begin, size in chunks:
                place = out.at[pl.ds(put, size), pl.ds(0, side)]
                moves.append(pltpu.make_async_copy(acc.at[pl.ds(begin, size)], place, out_sems.at[len(moves)]))
                put += size
        for move in moves:
            move.start()
        begin = jnp.zeros((32, side), jnp.float32), jnp.zeros((32, side), psi.dtype)
        total, m = lax.fori_loop(0, psi.shape[0], add, begin)
        total = jnp.sum(total, axis=0, keepdims=True)
        vec[...] = vec_ref[...]
        vec[pl.ds(vec.shape[0] - 1, 1), :] = sum(total[:, c : c + 128] for c in range(0, side, 128))
        small = jnp.sum(vec[...], axis=1, keepdims=True)
        digits = jnp.floor(small * digit_ref[0] + 0.5) - digit * jnp.floor(small * digit_ref[1] + 0.5)

        digits_ref[...] = digits
        for out in outs:
            rows = out.shape[1] - side

            def under(i, carry):
                out[i, pl.ds(side, rows), :] = jnp.zeros((rows, side), jnp.float32)
                out[i, pl.ds(side, vec.shape[0]), pl.ds(0, 128)] = digits
                return carry

            lax.fori_loop(0, out.shape[0], under, 0)
        bound = jnp.full((1, 128), limit * jnp.max(m.astype(jnp.float32)))
        power = jnp.clip(15.0 - jnp.ceil(jnp.log2(jnp.maximum(bound, 1e-30))), -60.0, 90.0)
        scales[...] = jnp.zeros_like(scales)
        scales[0:1, :] = jnp.exp2(power)
        scales[1:2, :] = 1.0 / jnp.exp2(power)
        for move in moves:
            move.wait()


def combine_kernel(slots, acc, other, scales, digits, *outs):
    side = acc.shape[2]
    at = 0
    for out in outs:
        for i in range(out.shape[0]):
            out[i, 0:side] = (acc[slots[at]] + other[at, 0:side]) * scales[0:1, 0:1]
            if out.shape[1] > side:
                out[i, side:] = other[at, side:]
                out[i, pl.ds(side, digits.shape[0]), pl.ds(0, 128)] += digits[...]
            at += 1


def finish_kernel(lower, digit_ref, scales, home, r0, r1, l0, l1, lower_ref, psi_ref, residual, ritz):
    side = psi_ref.shape[1]
    part = r0.shape[0]
    rows = -(-(2 * lower + 2) // 8) * 8
    place = (0, pl.ds(side, rows), pl.ds(0, 128))
    sums = jnp.sum((home[place] + r0[place] + l0[place]) * digit_ref[2], axis=1, keepdims=True)
    correlation = [sums[j : j + 1] for j in range(lower)]
    coeffs = [correlation[j] / sums[lower + j : lower + j + 1] for j in range(lower)]
    shifted = shift_energy * sum(c * x for c, x in zip(coeffs, correlation))
    value = (sums[rows - 1 : rows] + shifted) / sums[2 * lower : 2 * lower + 1]
    ritz[0] = jnp.sum(value)
    for s in range(psi_ref.shape[0]):
        r, l, at = (r0, l0, s) if s < part else (r1, l1, s - part)
        sigma = (home[s, 0:side] + r[at, 0:side] + l[at, 0:side]) * scales[1:2, 0:1]
        low = sum(c * lower_ref[j, s].astype(jnp.float32) for j, c in enumerate(coeffs))
        residual[s] = sigma + shift_energy * low - value * psi_ref[s].astype(jnp.float32)


def make_per_device(mesh):
    devices = mesh.shape["sector"]
    ring = ring_of(mesh)
    chips = len(ring)
    reach = chips // 2
    rows_y = 2 if mesh.shape["groups"] == 2 else 1

    def shift(by):
        return [
            (ring[p] * CORES + c, ring[(p + by) % chips] * CORES + c) for p in range(chips) for c in range(CORES)
        ]

    to_right, to_left = shift(1), shift(-1)

    def right(x):
        return lax.ppermute(x, "sector", to_right)

    def left(x):
        return lax.ppermute(x, "sector", to_left)

    def pair(x, hop):
        return lax.ppermute(x, "sector", [(i, i ^ hop) for i in range(devices)])

    def across(x):
        return pair(x, 1)

    def per_device(wavefunction, lower_states, left_env, right_env, term_list):
        per, side, _ = wavefunction.shape
        terms = left_env.shape[0]
        sectors = per * devices
        part = per // 2
        lower = lower_states.shape[0]
        base = chips * per
        tie = lax.optimization_barrier
        me = lax.axis_index("sector")

        keep = dict(compiler_params=pltpu.CompilerParams(vmem_limit_bytes=9 * 1024 * 1024))
        stages = reach + 1
        cap = (terms + stages * (BATCH - 1) + BATCH - 1) // BATCH * BATCH
        groups = next(g for g in (4, 2, 1) if terms % g == 0)
        vec_rows = -(-(2 * lower + 2) // 8) * 8
        left_hbm, right_hbm, psi_hbm, lower_hbm, list_hbm = [
            pltpu.with_memory_space_constraint(x, pltpu.HBM)
            for x in (left_env, right_env, wavefunction, lower_states, term_list.T)
        ]
        vec_shape = jax.ShapeDtypeStruct((vec_rows, 128), jnp.float32)
        row_shape = jax.ShapeDtypeStruct((8, 128), jnp.float32)
        tall = side + -(-vec_rows // 16) * 16
        acc_shape = pltpu.VMEM((sectors + 1, side, side), jnp.float32)
        digit_bits = 12 - (devices.bit_length() - 1)
        weights = np.zeros((3, vec_rows, 128), np.float32)
        for n in range(144 // digit_bits):
            weight = 2.0 ** (digit_bits * n - 72)
            weights[0, :, n], weights[1, :, n], weights[2, :, n] = 1 / weight, 2.0**-digit_bits / weight, weight
        weights = jnp.asarray(weights)
        psi_shape = pltpu.VMEM((sectors, side, side), wavefunction.dtype)

        def make_plan():
            return pl.pallas_call(
                functools.partial(plan_kernel, (chips, rows_y, per, cap, sectors)),
                in_specs=[INHBM, SCALAR, INHBM, INHBM, INHBM],
                out_specs=[KEEP] * 4 + [SCALAR] * 2,
                out_shape=[
                    pltpu.VMEM(left_env.shape, left_env.dtype),
                    vec_shape,
                    acc_shape,
                    psi_shape,
                    jax.ShapeDtypeStruct((cap,), jnp.int32),
                    jax.ShapeDtypeStruct((stages + 1,), jnp.int32),
                ],
                scratch_shapes=[
                    pltpu.SMEM((2, terms), jnp.int32),
                    pltpu.VMEM(wavefunction.shape, wavefunction.dtype),
                    pltpu.VMEM(lower_states.shape, lower_states.dtype),
                    pltpu.SMEM((terms,), jnp.int32),
                    pltpu.SMEM((terms,), jnp.int32),
                    pltpu.SMEM((stages,), jnp.int32),
                    pltpu.SemaphoreType.DMA((3,)),
                    pltpu.SemaphoreType.DMA((groups,)),
                ],
                cost_estimate=pl.CostEstimate(flops=0, bytes_accessed=12 << 20, transcendentals=0),
                **keep,
            )(list_hbm, me.reshape(1).astype(jnp.int32), psi_hbm, lower_hbm, left_hbm)

        route = [(reach, 0)] + [(d, h) for d in range(reach - 1, 0, -1) for h in (1, 0)]
        route_left = [(-d if d < reach else reach, 1 - h) for d, h in route]
        need = [x for both in zip(route, route_left) for x in both] + [(0, 0), (0, 1)]
        sets = [need[:4], need[4:]]

        def run_stage(stage, pieces, starts, acc, psi, vec=None):
            finish, sizes, more, small = [], [], [], []
            if stage == reach:
                finish = [[(base + rel % chips * per + h * part, part) for rel, h in parts] for parts in sets]
                sizes = [pltpu.VMEM((part * len(parts), tall, side), jnp.float32) for parts in sets]
                more, small = [vec, weights], [row_shape, vec_shape]
            n, m = len(pieces), len(more)
            scratch = [pltpu.SemaphoreType.DMA((n,))]
            if finish:
                scratch = [pltpu.VMEM((vec_rows, 128), jnp.float32), pltpu.SemaphoreType.DMA((len(need),))] + scratch
            scratch += [
                pltpu.VMEM((SLOTS, BATCH, side, side), right_env.dtype),
                pltpu.SemaphoreType.DMA((SLOTS,)),
            ]
            limit = 1.02 * terms * devices * side * side * 0.375 * 0.0546875
            return pl.pallas_call(
                functools.partial(stage_kernel, stage, starts, finish, limit, 2.0**digit_bits),
                in_specs=[SCALAR, SCALAR, KEEP, INHBM] + [INHBM if x is psi_hbm else ANYWHERE for x in pieces]
                + [KEEP] * (m + 2),
                out_specs=[KEEP] * 2 + [KEEP] * len(sizes) + [KEEP] * len(small),
                out_shape=[acc_shape, psi_shape] + sizes + small,
                input_output_aliases={4 + n + m: 0, 5 + n + m: 1},
                scratch_shapes=scratch,
                cost_estimate=pl.CostEstimate(
                    flops=4 * side**3 * terms // stages, bytes_accessed=1 << 20, transcendentals=0
                ),
                **keep,
            )(plan, bounds, left_vmem, right_hbm, *pieces, *more, acc, psi)

        r, l, sib = right(wavefunction), left(wavefunction), across(wavefunction)
        left_vmem, vec, acc, psi, plan, bounds = make_plan()
        late, late_at = [psi_hbm, sib], [0, base]
        for s in range(1, reach + 1):
            r, l, acc, psi = tie((r, l, acc, psi))
            rel = [(chips - s) * per, s * per] if s < reach else [reach * per, reach * per + part]
            held, at = late + [r, l, across(r), across(l)], late_at + rel + [base + x for x in rel]
            late, late_at = [], []
            if s < reach - 1:
                r, l = right(r), left(l)
            elif s < reach:
                r, l = right(r[:part]), left(l[part:])
            if s < reach:
                acc, psi = run_stage(s, held, at, acc, psi)
        acc, psi, *others, scales, digits = run_stage(reach, held, at, acc, psi, vec)

        first = across(others[0])
        first, waiting = tie((first, others[1]))
        got = [first, across(waiting)]
        own = {}
        for parts, there in zip(sets, got):
            keys = [key for key in parts if key[0] != 0]
            shapes = [(part, side if half else tall, side) for _, half in keys]
            if len(keys) < len(parts):
                shapes.append((per, tall, side))
            slots = [rel % chips * per + h * part + i for rel, h in parts for i in range(part)]
            tiles = pl.pallas_call(
                functools.partial(combine_kernel, slots),
                in_specs=[KEEP] * 4,
                out_specs=[KEEP] * len(shapes),
                out_shape=[jax.ShapeDtypeStruct(shape, jnp.float32) for shape in shapes],
                cost_estimate=pl.CostEstimate(flops=0, bytes_accessed=1 << 20, transcendentals=0),
                **keep,
            )(acc, there, scales, digits)
            own.update(zip(keys, tiles))
            home = tiles[-1]

        went, sent = [], []
        for n, (here, there) in enumerate(zip(route, route_left)):
            to_r, to_l = own[here], own[there]
            if n >= 2:
                back, _ = tie((went[n - 2], sent[n - 1]))
                to_r, to_l = to_r + back[0].astype(jnp.float32), to_l + back[1].astype(jnp.float32)
            sent.append((to_r.astype(jnp.float16), to_l.astype(jnp.float16)))
            went.append((right(sent[n][0]), left(sent[n][1])))
        (r1, l0), (r0, l1) = went[-2], went[-1]
        arrived = [x.astype(jnp.float32) for x in (r0, r1, l0, l1)]
        residual, ritz_value = pl.pallas_call(
            functools.partial(finish_kernel, lower),
            in_specs=[KEEP] * 9,
            out_specs=[KEEP, SCALAR],
            out_shape=[
                jax.ShapeDtypeStruct((per, side, side), jnp.float32),
                jax.ShapeDtypeStruct((1,), jnp.float32),
            ],
            cost_estimate=pl.CostEstimate(flops=0, bytes_accessed=2 << 20, transcendentals=0),
            **keep,
        )(weights, scales, home, *arrived, lower_states, wavefunction)
        return (residual, ritz_value)

    return per_device


def solution(mesh):
    return jax.shard_map(
        make_per_device(mesh),
        mesh=mesh,
        in_specs=(
            P(("groups", "sector"), None, None),
            P(None, ("groups", "sector"), None, None),
            P(("groups", "sector"), None, None),
            P(("groups", "sector"), None, None),
            P(("groups", "sector"), None),
        ),
        out_specs=(P(("groups", "sector"), None, None), P("groups")),
        check_vma=False,
    )
```
